32 devices in a mesh: rep: 16 (over z, x, core), fsdp: 2 (over y).
Axes of the slice: x: 2, y: 2, z: 4, core: 2. Of those that a mesh axis runs over, the one named last changes fastest.
Arguments:
- activations: bfloat16 [8192, 4096], P(('rep', 'fsdp')), may hold values from -6 to 6
- cotangent: bfloat16 [8192, 512], P(('rep', 'fsdp')), may hold values from -0.25 to 0.25
- momentum: bfloat16 [16, 4096, 512], P('rep', 'fsdp'), may hold values from -6 to 6
Outputs:
- new_momentum: bfloat16 [16, 4096, 512], P('rep', 'fsdp')
- update: bfloat16 [4096, 512], P('fsdp')
The draws below stay inside these ranges and needn't reach their ends.
All inputs are finite; a program needn't handle non-finite values.
Results may differ from the reference program's by a relative error of at most 0.001.
Values may be sent and summed in bfloat16 or wider, within the bound.
A program may use at most 64 MiB of HBM per device.

```python
import math
import jax
import jax.numpy as jnp
from jax import lax

ROWS = 4096
COLS = 512
TOK_DEV = 256
BLOCK = 64
KEEP = 16
TOKENS = 8192
N_REP = 16
N_FSDP = 2


def steps_of(stream_key, shape, cuts, least, high):
    def one(axis_at, blocks):
        draws = jax.random.uniform(jax.random.fold_in(jax.random.fold_in(stream_key, 6), axis_at), (blocks,), jnp.float32, least / len(cuts), high / len(cuts))
        return jnp.repeat(jnp.exp(draws), shape[axis_at] // blocks).reshape((-1,) + (1,) * (len(shape) - axis_at - 1))

    level = one(*cuts[0])
    for cut in cuts[1:]:
        level = level * one(*cut)
    return level


def noise(stream_key, dims, scale, bound, shards=(), kind=jnp.bfloat16):
    array = jax.random.normal(stream_key, dims, jnp.float32) * scale
    if len(shards) > 0:
        array = steps_of(stream_key, dims, shards, -0.22, 0.18) * array
    return jnp.clip(array, min=-bound, max=bound).astype(kind)


def setup_inputs(seed: int = 0) -> dict:
    key_of = jax.random.split(jax.random.key(seed), 4)
    return {
        "activations": noise(key_of[0], (TOKENS, ROWS), 1.0, 6.0, ((0, 32),)),
        "cotangent": noise(key_of[1], (TOKENS, COLS), (1.0 / (TOK_DEV * N_FSDP) ** 0.5), 0.25, ((0, 32),)),
        "momentum": noise(key_of[2], (N_REP, ROWS, COLS), 1.0, 6.0, ((0, 16), (1, 2))),
    }


def dct_basis():
    freq = jnp.arange(KEEP, dtype=jnp.float32)[:, None]
    place = jnp.arange(BLOCK, dtype=jnp.float32)[None, :]
    table = math.sqrt(2.0 / BLOCK) * jnp.cos(math.pi * (2.0 * place + 1.0) * freq / (2.0 * BLOCK))
    return jnp.where(freq == 0.0, table * math.sqrt(0.5), table)

def analyze(matrix, basis_rows):
    row_count, col_count = matrix.shape
    blocks = matrix.reshape(row_count // BLOCK, BLOCK, col_count // BLOCK, BLOCK)
    halfway = jnp.einsum('kr,arbc->akbc', basis_rows, blocks, precision=lax.Precision.HIGHEST)
    result = jnp.einsum('akbc,lc->akbl', halfway, basis_rows, precision=lax.Precision.HIGHEST)
    return result.reshape(row_count // BLOCK, KEEP, col_count // BLOCK * KEEP)

def synthesize(coefficients, basis_rows):
    row_blocks, keep_rows, wide = coefficients.shape
    col_blocks = wide // KEEP
    shaped = coefficients.reshape(row_blocks, KEEP, col_blocks, KEEP)
    halfway = jnp.einsum('akbl,lc->akbc', shaped, basis_rows, precision=lax.Precision.HIGHEST)
    blocks = jnp.einsum('kr,akbc->arbc', basis_rows, halfway, precision=lax.Precision.HIGHEST)
    return blocks.reshape(row_blocks * BLOCK, col_blocks * BLOCK)

def reference(activations, cotangent, momentum):
    tokens_rep = TOK_DEV * N_FSDP
    basis_rows = dct_basis()

    def replica_accum(replica):
        start = (replica * tokens_rep).astype(jnp.int32)
        inputs = lax.dynamic_slice_in_dim(activations, start, tokens_rep, 0)
        grads = lax.dynamic_slice_in_dim(cotangent, start, tokens_rep, 0)
        gradient = lax.dot_general(inputs, grads, (((0,), (0,)), ((), ())), preferred_element_type=jnp.float32)
        return 0.999 * momentum[replica].astype(jnp.float32) + gradient
    accum_all = lax.map(replica_accum, jnp.arange(N_REP, dtype=jnp.int32))
    coef_all = lax.map(lambda matrix: analyze(matrix, basis_rows), accum_all)
    mean_coefficients = lax.optimization_barrier(jnp.sum(coef_all, axis=0)) / N_REP
    recon = synthesize(mean_coefficients, basis_rows)
    new_momentum = (accum_all - recon[None]).astype(jnp.bfloat16)
    scale_inv = lax.rsqrt(jnp.mean(recon * recon) + 1e-06)
    update = (recon * scale_inv).astype(jnp.bfloat16)
    return (new_momentum, update)
```

```python
import functools
import math

import jax
import jax.numpy as jnp
import numpy as np
from jax import lax
from jax.experimental import pallas as pl
from jax.experimental.pallas import tpu as pltpu
from jax.sharding import PartitionSpec as P

BLOCK = 64
KEEP = 16
CHUNK = 256
FIRST = 4
MESH = pl.DeviceIdType.MESH
F32 = jnp.float32
BF16 = jnp.bfloat16


def dct_basis():
    freq = jnp.arange(KEEP, dtype=jnp.float32)[:, None]
    place = jnp.arange(BLOCK, dtype=jnp.float32)[None, :]
    table = math.sqrt(2.0 / BLOCK) * jnp.cos(math.pi * (2.0 * place + 1.0) * freq / (2.0 * BLOCK))
    return jnp.where(freq == 0.0, table * math.sqrt(0.5), table)


def analyze(matrix, basis_rows):
    row_count, col_count = matrix.shape
    blocks = matrix.reshape(row_count // BLOCK, BLOCK, col_count // BLOCK, BLOCK)
    halfway = jnp.einsum("kr,arbc->akbc", basis_rows, blocks, precision=lax.Precision.HIGHEST)
    result = jnp.einsum("akbc,lc->akbl", halfway, basis_rows, precision=lax.Precision.HIGHEST)
    return result.reshape(row_count // BLOCK, KEEP, col_count // BLOCK * KEEP)


def synthesize(coefficients, basis_rows):
    row_blocks, keep_rows, wide = coefficients.shape
    col_blocks = wide // KEEP
    shaped = coefficients.reshape(row_blocks, KEEP, col_blocks, KEEP)
    halfway = jnp.einsum("akbl,lc->akbc", shaped, basis_rows, precision=lax.Precision.HIGHEST)
    blocks = jnp.einsum("kr,akbc->arbc", basis_rows, halfway, precision=lax.Precision.HIGHEST)
    return blocks.reshape(row_blocks * BLOCK, col_blocks * BLOCK)


def token_product(inputs, grads):
    return lax.dot_general(
        inputs, grads, (((0,), (0,)), ((), ())), preferred_element_type=jnp.float32
    )


def plain_body(activations, cotangent, momentum):
    rows_dev = momentum.shape[1]
    col_count = momentum.shape[2]
    groups = lax.axis_size("fsdp")
    features = lax.all_to_all(activations, "fsdp", split_axis=1, concat_axis=0, tiled=True)
    grads = lax.all_gather(cotangent, "fsdp", axis=0, tiled=True)
    gradient = token_product(features, grads)
    accum = 0.999 * momentum[0].astype(jnp.float32) + gradient
    basis_rows = dct_basis()
    local_coef = analyze(accum, basis_rows)
    summed = lax.psum(local_coef, "rep")
    mean_coefficients = summed / lax.axis_size("rep")
    recon = synthesize(mean_coefficients, basis_rows)
    squares = lax.psum(jnp.sum(recon * recon), "fsdp")
    scale_inv = lax.rsqrt(squares / (rows_dev * groups * col_count) + 1e-06)
    update = (recon * scale_inv).astype(jnp.bfloat16)
    new_momentum = (accum - recon).astype(jnp.bfloat16)[None]
    return (new_momentum, update)


def tables(cols):
    freq = np.arange(KEEP, dtype=np.float64)[:, None]
    place = np.arange(BLOCK, dtype=np.float64)[None, :]
    basis = math.sqrt(2.0 / BLOCK) * np.cos(math.pi * (2.0 * place + 1.0) * freq / (2.0 * BLOCK))
    basis[0] *= math.sqrt(0.5)
    bf16 = np.dtype(jnp.bfloat16)

    def split(full):
        high = full.astype(bf16)
        low = (full - high.astype(np.float64)).astype(bf16)
        return high, low

    col_high, col_low = split(np.kron(np.eye(cols // BLOCK), basis))
    row_high, row_low = split(np.kron(np.eye(CHUNK // BLOCK), basis))
    col_in = np.concatenate([col_high.T, col_low.T], 1)
    row_in = np.concatenate([row_high, row_low], 0)
    col_out = np.concatenate([col_high, col_high, col_low], 0)
    row_out = np.concatenate([row_high.T, row_low.T, row_high.T, row_low.T], 1)
    return col_in, row_in, col_out, row_out


def halves(x):
    high = x.astype(BF16)
    low = (x - high.astype(F32)).astype(BF16)
    return high, low


def dot(a, b):
    return jnp.dot(a, b, preferred_element_type=F32)


def kernel(
    act, cot, mom, col_in, row_in, col_out, row_out,
    out_mom, out_upd,
    a_own, a_oth, a_recv, c_own, c_recv, c_coef, m_own, accum, mid,
    part, pair, parts, share, share_recv, gathered, upd, new,
    load_sem, out_sem, bulk_send, bulk_recv, cot_sem, pair_sem,
    rs_send, rs_recv, y_sem, ag_send, ag_recv, fw_send, fw_recv,
    *, n_rep, n_chunks, n_elems,
):
    nq = n_rep // 2
    rows = n_chunks * CHUNK
    kept = n_chunks * (CHUNK // BLOCK * KEEP)
    per_chunk = CHUNK // BLOCK * KEEP
    half = kept // 2
    piece = half // nq
    wide = part.shape[2]
    r = lax.axis_index("rep")
    f = lax.axis_index("fsdp")
    q = r // 2
    c = r % 2
    pal = 2 * q + (1 - c)
    opp = 1 - f

    def peer(d):
        return 2 * lax.rem(q + d, nq) + c

    barrier = pltpu.get_barrier_semaphore()
    targets = [(r, opp), (pal, f)] + [(peer(d), f) for d in range(1, nq)]
    for target in targets:
        pl.semaphore_signal(barrier, inc=1, device_id=target, device_id_type=MESH)

    own_cols = pl.ds(pl.multiple_of(f * rows, rows), rows)
    oth_cols = pl.ds(pl.multiple_of(opp * rows, rows), rows)
    loads = [
        pltpu.make_async_copy(cot, c_own, load_sem.at[0]),
        pltpu.make_async_copy(mom.at[0], m_own, load_sem.at[1]),
        pltpu.make_async_copy(act.at[:, own_cols], a_own, load_sem.at[2]),
        pltpu.make_async_copy(act.at[:, oth_cols], a_oth, load_sem.at[3]),
    ]
    for load in loads:
        load.start()

    def remote(src, dst, send, recv, target):
        return pltpu.make_async_remote_copy(
            src_ref=src, dst_ref=dst, send_sem=send, recv_sem=recv,
            device_id=target, device_id_type=MESH,
        )

    cot_copy = remote(cot, c_recv, cot_sem.at[0], cot_sem.at[1], (r, opp))
    bulk = []
    for k in range(n_chunks):
        cols = pl.ds(pl.multiple_of(opp * rows + k * CHUNK, CHUNK), CHUNK)
        bulk.append(remote(act.at[:, cols], a_recv.at[k], bulk_send.at[k], bulk_recv.at[k], (r, opp)))

    pl.semaphore_wait(barrier, len(targets))
    cot_copy.start()
    for k in range(min(FIRST, n_chunks)):
        bulk[k].start()

    loads[0].wait()
    proj = dot(c_own[...], col_in[...])
    high, low = halves(proj[:, :wide] + proj[:, wide:])
    c_coef[:, :wide] = high
    c_coef[:, wide:] = low

    def chunk_coefs(slot, h, g):
        hh, hl = halves(h)
        y = dot(row_in[...], jnp.concatenate([hh, hl], axis=1))
        y = y[:, :wide] + y[:, wide:]
        part[slot, pl.ds(pl.multiple_of(g * per_chunk, per_chunk), per_chunk), :] = y[:per_chunk] + y[per_chunk:]

    loads[1].wait()
    loads[2].wait()

    def own_step(g, carry):
        span = pl.ds(pl.multiple_of(g * CHUNK, CHUNK), CHUNK)
        h = token_product(a_own[:, span], c_coef[...])
        m = dot(m_own[span, :], col_in[...])
        h = h[:, :wide] + h[:, wide:] + 0.999 * (m[:, :wide] + m[:, wide:])
        chunk_coefs(0, h, g)
        return carry

    lax.fori_loop(0, n_chunks, own_step, 0)
    loads[3].wait()

    def oth_step(g, carry):
        span = pl.ds(pl.multiple_of(g * CHUNK, CHUNK), CHUNK)
        h = token_product(a_oth[:, span], c_coef[...])
        chunk_coefs(1, h[:, :wide] + h[:, wide:], g)
        return carry

    lax.fori_loop(0, n_chunks, oth_step, 0)

    pal_rows = pl.ds(pl.multiple_of((1 - c) * half, half), half)
    pair_copy = remote(part.at[:, pal_rows], pair, pair_sem.at[0], pair_sem.at[1], (pal, f))
    pair_copy.start()

    def grad_step(g, carry):
        span = pl.ds(pl.multiple_of(g * CHUNK, CHUNK), CHUNK)
        accum[span, :] = 0.999 * m_own[span, :].astype(F32) + token_product(a_own[:, span], c_own[...])
        return carry

    lax.fori_loop(0, n_chunks // 2, grad_step, 0)

    pair_copy.wait()
    my_rows = pl.ds(pl.multiple_of(c * half, half), half)
    pair[...] = pair[...] + part[:, my_rows, :]

    scatter = []
    for d in range(1, nq):
        at = pl.ds(pl.multiple_of(lax.rem(q + d, nq) * piece, piece), piece)
        copy = remote(pair.at[:, at], parts.at[d], rs_send.at[d], rs_recv.at[d], (peer(d), f))
        copy.start()
        scatter.append(copy)

    lax.fori_loop(n_chunks // 2, n_chunks, grad_step, 0)

    total = pair[:, pl.ds(pl.multiple_of(q * piece, piece), piece), :]
    for d in range(1, nq):
        scatter[d - 1].wait()
        total = total + parts[d]
    share[...] = total

    y_copy = remote(share, share_recv, y_sem.at[0], y_sem.at[1], (r, opp))
    y_copy.start()
    for k in range(min(FIRST, n_chunks), n_chunks):
        bulk[k].start()
    y_copy.wait()
    mine = (share[0] + share_recv[1]) / n_rep
    other = (share[1] + share_recv[0]) / n_rep
    squares = (mine * mine + other * other).reshape(piece // 8, 8, wide)
    gathered[c, q, :piece] = mine
    gathered[c, q, piece:] = jnp.sum(squares, axis=0)

    spread = []
    for d in range(1, nq):
        copy = remote(gathered.at[c, q], gathered.at[c, q], ag_send.at[d], ag_recv.at[d], (peer(d), f))
        copy.start()
        spread.append(copy)
    forward = []
    for d in range(nq):
        src = lax.rem(q - d + nq, nq)
        if d > 0:
            spread[d - 1].wait_recv()
        copy = remote(gathered.at[c, src], gathered.at[c, src], fw_send.at[d], fw_recv.at[d], (pal, f))
        copy.start()
        forward.append(copy)
    for d in range(nq):
        forward[d].wait()
        if d > 0:
            spread[d - 1].wait_send()

    everything = gathered[...]
    coefs = everything[:, :, :piece].reshape(kept, wide)
    sq = everything[:, :, piece:].reshape(n_rep * 8, wide)
    sq = jnp.sum(jnp.sum(sq, axis=0, keepdims=True), axis=1, keepdims=True)
    scale = lax.rsqrt(sq / n_elems + 1e-06)
    ch, cl = halves(coefs)
    mid[...] = dot(jnp.concatenate([ch, cl, ch], axis=1), col_out[...])

    def recon_step(g, carry):
        span = pl.ds(pl.multiple_of(g * CHUNK, CHUNK), CHUNK)
        x = mid[pl.ds(pl.multiple_of(g * per_chunk, per_chunk), per_chunk), :]
        xh, xl = halves(x)
        recon = dot(row_out[...], jnp.concatenate([xh, xh, xl, xl], axis=0))
        upd[span, :] = (recon * scale).astype(BF16)
        accum[span, :] = accum[span, :] - recon
        return carry

    lax.fori_loop(0, n_chunks, recon_step, 0)
    upd_out = pltpu.make_async_copy(upd, out_upd, out_sem.at[0])
    upd_out.start()

    cot_copy.wait()
    outs = []
    for k in range(n_chunks):
        bulk[k].wait()
        span = slice(k * CHUNK, (k + 1) * CHUNK)
        new[span, :] = (accum[span, :] + token_product(a_recv[k], c_recv[...])).astype(BF16)
        copy = pltpu.make_async_copy(new.at[span], out_mom.at[0, span], out_sem.at[k + 1])
        copy.start()
        outs.append(copy)
    upd_out.wait()
    for copy in outs:
        copy.wait()


def kernel_body(activations, cotangent, momentum):
    tokens = activations.shape[0]
    rows, cols = momentum.shape[1], momentum.shape[2]
    n_rep = lax.axis_size("rep")
    groups = lax.axis_size("fsdp")
    n_chunks = rows // CHUNK
    wide = cols // BLOCK * KEEP
    kept = rows // BLOCK * KEEP
    nq = n_rep // 2
    half = kept // 2
    piece = half // nq
    any_spec = pl.BlockSpec(memory_space=pl.ANY)
    vmem_spec = pl.BlockSpec(memory_space=pltpu.VMEM)
    dma = pltpu.SemaphoreType.DMA
    return pl.pallas_call(
        functools.partial(kernel, n_rep=n_rep, n_chunks=n_chunks, n_elems=rows * groups * cols),
        out_shape=(
            jax.ShapeDtypeStruct((1, rows, cols), BF16),
            jax.ShapeDtypeStruct((rows, cols), BF16),
        ),
        in_specs=[any_spec] * 3 + [vmem_spec] * 4,
        out_specs=(any_spec, any_spec),
        scratch_shapes=[
            pltpu.VMEM((tokens, rows), BF16),
            pltpu.VMEM((tokens, rows), BF16),
            pltpu.VMEM((n_chunks, tokens, CHUNK), BF16),
            pltpu.VMEM((tokens, cols), BF16),
            pltpu.VMEM((tokens, cols), BF16),
            pltpu.VMEM((tokens, 2 * wide), BF16),
            pltpu.VMEM((rows, cols), BF16),
            pltpu.VMEM((rows, cols), F32),
            pltpu.VMEM((kept, cols), F32),
            pltpu.VMEM((2, kept, wide), F32),
            pltpu.VMEM((2, half, wide), F32),
            pltpu.VMEM((nq, 2, piece, wide), F32),
            pltpu.VMEM((2, piece, wide), F32),
            pltpu.VMEM((2, piece, wide), F32),
            pltpu.VMEM((2, nq, piece + 8, wide), F32),
            pltpu.VMEM((rows, cols), BF16),
            pltpu.VMEM((rows, cols), BF16),
            dma((4,)),
            dma((n_chunks + 1,)),
            dma((n_chunks,)),
            dma((n_chunks,)),
            dma((2,)),
            dma((2,)),
            dma((nq,)),
            dma((nq,)),
            dma((2,)),
            dma((nq,)),
            dma((nq,)),
            dma((nq,)),
            dma((nq,)),
        ],
        compiler_params=pltpu.CompilerParams(
            collective_id=0, has_side_effects=True, vmem_limit_bytes=48 * 2**20
        ),
    )(activations, cotangent, momentum, *(jnp.asarray(t) for t in tables(cols)))


def body(activations, cotangent, momentum):
    n_rep = lax.axis_size("rep")
    rows, cols = momentum.shape[1], momentum.shape[2]
    wide = cols // BLOCK * KEEP
    kept = rows // BLOCK * KEEP
    fits = (
        lax.axis_size("fsdp") == 2
        and n_rep % 2 == 0
        and kept % (8 * n_rep) == 0
        and rows % CHUNK == 0
        and wide % 128 == 0
        and activations.shape[0] % 128 == 0
    )
    return (kernel_body if fits else plain_body)(activations, cotangent, momentum)


def solution(mesh):
    placed = (P(("rep", "fsdp"), None), P(("rep", "fsdp"), None), P("rep", "fsdp", None))
    return jax.shard_map(
        body,
        mesh=mesh,
        in_specs=placed,
        out_specs=(P("rep", "fsdp", None), P("fsdp", None)),
        check_vma=False,
    )
```

```python
import functools
import math

import jax
import jax.numpy as jnp
from jax import lax
from jax.experimental import pallas as pl
from jax.experimental.pallas import tpu as pltpu
from jax.sharding import PartitionSpec as P

BLOCK = 64
KEEP = 16
CHUNK = 256
FIRST = 4
MESH = pl.DeviceIdType.MESH
F32 = jnp.float32
BF16 = jnp.bfloat16


def dct_basis():
    freq = jnp.arange(KEEP, dtype=jnp.float32)[:, None]
    place = jnp.arange(BLOCK, dtype=jnp.float32)[None, :]
    table = math.sqrt(2.0 / BLOCK) * jnp.cos(math.pi * (2.0 * place + 1.0) * freq / (2.0 * BLOCK))
    return jnp.where(freq == 0.0, table * math.sqrt(0.5), table)


def analyze(matrix, basis_rows):
    row_count, col_count = matrix.shape
    blocks = matrix.reshape(row_count // BLOCK, BLOCK, col_count // BLOCK, BLOCK)
    halfway = jnp.einsum("kr,arbc->akbc", basis_rows, blocks, precision=lax.Precision.HIGHEST)
    result = jnp.einsum("akbc,lc->akbl", halfway, basis_rows, precision=lax.Precision.HIGHEST)
    return result.reshape(row_count // BLOCK, KEEP, col_count // BLOCK * KEEP)


def synthesize(coefficients, basis_rows):
    row_blocks, keep_rows, wide = coefficients.shape
    col_blocks = wide // KEEP
    shaped = coefficients.reshape(row_blocks, KEEP, col_blocks, KEEP)
    halfway = jnp.einsum("akbl,lc->akbc", shaped, basis_rows, precision=lax.Precision.HIGHEST)
    blocks = jnp.einsum("kr,akbc->arbc", basis_rows, halfway, precision=lax.Precision.HIGHEST)
    return blocks.reshape(row_blocks * BLOCK, col_blocks * BLOCK)


def token_product(inputs, grads):
    return lax.dot_general(
        inputs, grads, (((0,), (0,)), ((), ())), preferred_element_type=jnp.float32
    )


def plain_body(activations, cotangent, momentum):
    rows_dev = momentum.shape[1]
    col_count = momentum.shape[2]
    groups = lax.axis_size("fsdp")
    features = lax.all_to_all(activations, "fsdp", split_axis=1, concat_axis=0, tiled=True)
    grads = lax.all_gather(cotangent, "fsdp", axis=0, tiled=True)
    gradient = token_product(features, grads)
    accum = 0.999 * momentum[0].astype(jnp.float32) + gradient
    basis_rows = dct_basis()
    local_coef = analyze(accum, basis_rows)
    summed = lax.psum(local_coef, "rep")
    mean_coefficients = summed / lax.axis_size("rep")
    recon = synthesize(mean_coefficients, basis_rows)
    squares = lax.psum(jnp.sum(recon * recon), "fsdp")
    scale_inv = lax.rsqrt(squares / (rows_dev * groups * col_count) + 1e-06)
    update = (recon * scale_inv).astype(jnp.bfloat16)
    new_momentum = (accum - recon).astype(jnp.bfloat16)[None]
    return (new_momentum, update)


def block_basis(kept, full):
    k = lax.broadcasted_iota(jnp.int32, (kept, full), 0)
    n = lax.broadcasted_iota(jnp.int32, (kept, full), 1)
    freq = k & (KEEP - 1)
    turn = ((2 * (n & (BLOCK - 1)) + 1) * freq) & (4 * BLOCK - 1)
    table = math.sqrt(2.0 / BLOCK) * jnp.cos(turn.astype(F32) * (math.pi / (2.0 * BLOCK)))
    table = jnp.where(freq == 0, math.sqrt(1.0 / BLOCK), table)
    inside = (k >> int(math.log2(KEEP))) == (n >> int(math.log2(BLOCK)))
    return halves(jnp.where(inside, table, 0.0))


def halves(x):
    high = x.astype(BF16)
    low = (x - high.astype(F32)).astype(BF16)
    return high, low


def dot(a, b):
    return jnp.dot(a, b, preferred_element_type=F32)


def dot_rows(a, b):
    return lax.dot_general(a, b, (((1,), (1,)), ((), ())), preferred_element_type=F32)


def kernel(
    act, cot, mom,
    new, upd,
    a_own, a_oth, a_recv, c_own, c_recv, c_coef, m_own, accum, mid,
    part, pair, parts, share, share_recv, gathered,
    col_basis, row_in, row_out,
    load_sem, bulk_send, bulk_recv, cot_sem, pair_sem,
    rs_send, rs_recv, y_sem, ag_send, ag_recv, fw_send, fw_recv,
    *, n_rep, n_chunks, n_elems,
):
    nq = n_rep // 2
    rows = n_chunks * CHUNK
    kept = n_chunks * (CHUNK // BLOCK * KEEP)
    per_chunk = CHUNK // BLOCK * KEEP
    half = kept // 2
    piece = half // nq
    wide = part.shape[2]
    r = lax.axis_index("rep")
    f = lax.axis_index("fsdp")
    q = r // 2
    c = r % 2
    pal = 2 * q + (1 - c)
    opp = 1 - f

    def peer(d):
        return 2 * lax.rem(q + d, nq) + c

    barrier = pltpu.get_barrier_semaphore()
    targets = [(r, opp), (pal, f)] + [(peer(d), f) for d in range(1, nq)]
    for target in targets:
        pl.semaphore_signal(barrier, inc=1, device_id=target, device_id_type=MESH)

    own_cols = pl.ds(pl.multiple_of(f * rows, rows), rows)
    oth_cols = pl.ds(pl.multiple_of(opp * rows, rows), rows)
    loads = [
        pltpu.make_async_copy(cot, c_own, load_sem.at[0]),
        pltpu.make_async_copy(mom.at[0], m_own, load_sem.at[1]),
        pltpu.make_async_copy(act.at[:, own_cols], a_own, load_sem.at[2]),
        pltpu.make_async_copy(act.at[:, oth_cols], a_oth, load_sem.at[3]),
    ]
    for at in (0, 2, 1, 3):
        loads[at].start()

    def remote(src, dst, send, recv, target):
        return pltpu.make_async_remote_copy(
            src_ref=src, dst_ref=dst, send_sem=send, recv_sem=recv,
            device_id=target, device_id_type=MESH,
        )

    cot_copy = remote(cot, c_recv, cot_sem.at[0], cot_sem.at[1], (r, opp))
    bulk = []
    for k in range(n_chunks):
        cols = pl.ds(pl.multiple_of(opp * rows + k * CHUNK, CHUNK), CHUNK)
        bulk.append(remote(act.at[:, cols], a_recv.at[k], bulk_send.at[k], bulk_recv.at[k], (r, opp)))

    col_high, col_low = block_basis(wide, col_basis.shape[1])
    col_basis[:wide] = col_high
    col_basis[wide : 2 * wide] = col_high
    col_basis[2 * wide :] = col_low
    row_high, row_low = block_basis(per_chunk, CHUNK)
    row_in[:per_chunk] = row_high
    row_in[per_chunk:] = row_low
    row_out[...] = jnp.concatenate([row_high, row_low, row_high, row_low], axis=0).T

    pl.semaphore_wait(barrier, len(targets))
    cot_copy.start()
    for k in range(min(FIRST, n_chunks)):
        bulk[k].start()

    loads[0].wait()
    proj = dot_rows(c_own[...], col_basis[wide:])
    high, low = halves(proj[:, :wide] + proj[:, wide:])
    c_coef[:, :wide] = high
    c_coef[:, wide:] = low

    def chunk_coefs(slot, h, g):
        hh, hl = halves(h)
        y = dot(row_in[...], jnp.concatenate([hh, hl], axis=1))
        y = y[:, :wide] + y[:, wide:]
        part[slot, pl.ds(pl.multiple_of(g * per_chunk, per_chunk), per_chunk), :] = y[:per_chunk] + y[per_chunk:]

    loads[1].wait()
    loads[2].wait()

    def own_step(g, carry):
        span = pl.ds(pl.multiple_of(g * CHUNK, CHUNK), CHUNK)
        h = token_product(a_own[:, span], c_coef[...])
        m = dot_rows(m_own[span, :], col_basis[wide:])
        h = h[:, :wide] + h[:, wide:] + 0.999 * (m[:, :wide] + m[:, wide:])
        chunk_coefs(0, h, g)
        return carry

    lax.fori_loop(0, n_chunks, own_step, 0)
    loads[3].wait()

    def oth_step(g, carry):
        span = pl.ds(pl.multiple_of(g * CHUNK, CHUNK), CHUNK)
        h = token_product(a_oth[:, span], c_coef[...])
        chunk_coefs(1, h[:, :wide] + h[:, wide:], g)
        return carry

    lax.fori_loop(0, n_chunks, oth_step, 0)

    pal_rows = pl.ds(pl.multiple_of((1 - c) * half, half), half)
    pair_copy = remote(part.at[:, pal_rows], pair, pair_sem.at[0], pair_sem.at[1], (pal, f))
    pair_copy.start()

    def grad_step(g, carry):
        span = pl.ds(pl.multiple_of(g * CHUNK, CHUNK), CHUNK)
        accum[span, :] = 0.999 * m_own[span, :].astype(F32) + token_product(a_own[:, span], c_own[...])
        return carry

    lax.fori_loop(0, n_chunks // 2, grad_step, 0)

    pair_copy.wait()
    my_rows = pl.ds(pl.multiple_of(c * half, half), half)
    pair[...] = pair[...] + part[:, my_rows, :]

    scatter = []
    for d in range(1, nq):
        at = pl.ds(pl.multiple_of(lax.rem(q + d, nq) * piece, piece), piece)
        copy = remote(pair.at[:, at], parts.at[d], rs_send.at[d], rs_recv.at[d], (peer(d), f))
        copy.start()
        scatter.append(copy)

    lax.fori_loop(n_chunks // 2, n_chunks, grad_step, 0)

    total = pair[:, pl.ds(pl.multiple_of(q * piece, piece), piece), :]
    for d in range(1, nq):
        scatter[d - 1].wait()
        total = total + parts[d]
    share[...] = total

    y_copy = remote(share, share_recv, y_sem.at[0], y_sem.at[1], (r, opp))
    y_copy.start()
    for k in range(min(FIRST, n_chunks), n_chunks):
        bulk[k].start()
    y_copy.wait()
    mine = (share[0] + share_recv[1]) / n_rep
    other = (share[1] + share_recv[0]) / n_rep
    squares = (mine * mine + other * other).reshape(piece // 8, 8, wide)
    gathered[c, q, :piece] = mine
    gathered[c, q, piece:] = jnp.sum(squares, axis=0)

    spread = []
    for d in range(1, nq):
        copy = remote(gathered.at[c, q], gathered.at[c, q], ag_send.at[d], ag_recv.at[d], (peer(d), f))
        copy.start()
        spread.append(copy)
    forward = []
    for d in range(nq):
        src = lax.rem(q - d + nq, nq)
        if d > 0:
            spread[d - 1].wait_recv()
        copy = remote(gathered.at[c, src], gathered.at[c, src], fw_send.at[d], fw_recv.at[d], (pal, f))
        copy.start()
        forward.append(copy)
    for d in range(nq):
        forward[d].wait()
        if d > 0:
            spread[d - 1].wait_send()

    everything = gathered[...]
    coefs = everything[:, :, :piece].reshape(kept, wide)
    sq = everything[:, :, piece:].reshape(n_rep * 8, wide)
    sq = jnp.sum(jnp.sum(sq, axis=0, keepdims=True), axis=1, keepdims=True)
    scale = lax.rsqrt(sq / n_elems + 1e-06)
    ch, cl = halves(coefs)
    mid[...] = dot(jnp.concatenate([ch, cl, ch], axis=1), col_basis[...])

    def recon_step(g, carry):
        span = pl.ds(pl.multiple_of(g * CHUNK, CHUNK), CHUNK)
        x = mid[pl.ds(pl.multiple_of(g * per_chunk, per_chunk), per_chunk), :]
        xh, xl = halves(x)
        recon = dot(row_out[...], jnp.concatenate([xh, xh, xl, xl], axis=0))
        upd[span, :] = (recon * scale).astype(BF16)
        accum[span, :] = accum[span, :] - recon
        return carry

    lax.fori_loop(0, n_chunks, recon_step, 0)
    cot_copy.wait()
    for k in range(n_chunks):
        bulk[k].wait()
        span = slice(k * CHUNK, (k + 1) * CHUNK)
        new[0, span, :] = (accum[span, :] + token_product(a_recv[k], c_recv[...])).astype(BF16)


def kernel_body(activations, cotangent, momentum):
    tokens = activations.shape[0]
    rows, cols = momentum.shape[1], momentum.shape[2]
    n_rep = lax.axis_size("rep")
    groups = lax.axis_size("fsdp")
    n_chunks = rows // CHUNK
    wide = cols // BLOCK * KEEP
    kept = rows // BLOCK * KEEP
    per_chunk = CHUNK // BLOCK * KEEP
    nq = n_rep // 2
    half = kept // 2
    piece = half // nq
    hbm_spec = pl.BlockSpec(memory_space=pltpu.HBM)
    vmem_spec = pl.BlockSpec(memory_space=pltpu.VMEM)
    dma = pltpu.SemaphoreType.DMA
    return pl.pallas_call(
        functools.partial(kernel, n_rep=n_rep, n_chunks=n_chunks, n_elems=rows * groups * cols),
        out_shape=(
            jax.ShapeDtypeStruct((1, rows, cols), BF16),
            jax.ShapeDtypeStruct((rows, cols), BF16),
        ),
        in_specs=[hbm_spec] * 3,
        out_specs=(vmem_spec, vmem_spec),
        scratch_shapes=[
            pltpu.VMEM((tokens, rows), BF16),
            pltpu.VMEM((tokens, rows), BF16),
            pltpu.VMEM((n_chunks, tokens, CHUNK), BF16),
            pltpu.VMEM((tokens, cols), BF16),
            pltpu.VMEM((tokens, cols), BF16),
            pltpu.VMEM((tokens, 2 * wide), BF16),
            pltpu.VMEM((rows, cols), BF16),
            pltpu.VMEM((rows, cols), F32),
            pltpu.VMEM((kept, cols), F32),
            pltpu.VMEM((2, kept, wide), F32),
            pltpu.VMEM((2, half, wide), F32),
            pltpu.VMEM((nq, 2, piece, wide), F32),
            pltpu.VMEM((2, piece, wide), F32),
            pltpu.VMEM((2, piece, wide), F32),
            pltpu.VMEM((2, nq, piece + 8, wide), F32),
            pltpu.VMEM((3 * wide, cols), BF16),
            pltpu.VMEM((2 * per_chunk, CHUNK), BF16),
            pltpu.VMEM((CHUNK, 4 * per_chunk), BF16),
            dma((4,)),
            dma((n_chunks,)),
            dma((n_chunks,)),
            dma((2,)),
            dma((2,)),
            dma((nq,)),
            dma((nq,)),
            dma((2,)),
            dma((nq,)),
            dma((nq,)),
            dma((nq,)),
            dma((nq,)),
        ],
        compiler_params=pltpu.CompilerParams(
            collective_id=0, has_side_effects=True, vmem_limit_bytes=48 * 2**20
        ),
    )(activations, cotangent, momentum)


def body(activations, cotangent, momentum):
    n_rep = lax.axis_size("rep")
    rows, cols = momentum.shape[1], momentum.shape[2]
    wide = cols // BLOCK * KEEP
    kept = rows // BLOCK * KEEP
    fits = (
        lax.axis_size("fsdp") == 2
        and n_rep % 2 == 0
        and kept % (8 * n_rep) == 0
        and rows % CHUNK == 0
        and wide % 128 == 0
        and activations.shape[0] % 128 == 0
    )
    return (kernel_body if fits else plain_body)(activations, cotangent, momentum)


def solution(mesh):
    placed = (P(("rep", "fsdp"), None), P(("rep", "fsdp"), None), P("rep", "fsdp", None))
    return jax.shard_map(
        body,
        mesh=mesh,
        in_specs=placed,
        out_specs=(P("rep", "fsdp", None), P("fsdp", None)),
        check_vma=False,
    )
```
